32 devices in a mesh: groups: 1, expert: 8 (over z, y), dp: 4 (over x, core).
Axes of the slice: x: 2, y: 2, z: 4, core: 2. Of those that a mesh axis runs over, the one named last changes fastest.
Arguments:
- tokens: bfloat16 [256, 4096], P(('groups', 'expert', 'dp')), may hold values from -6 to 6
- norm_gain: float32 [4096], replicated, may hold values from 0.1 to 1.9
- gate_weight: bfloat16 [32, 4096, 384], P(('expert', 'dp')), may hold values from -0.09375 to 0.09375
- up_weight: bfloat16 [32, 4096, 384], P(('expert', 'dp')), may hold values from -0.09375 to 0.09375
- down_weight: bfloat16 [32, 384, 4096], P(('expert', 'dp')), may hold values from -0.21875 to 0.21875
- experts_chosen: int32 [256, 8], P(('groups', 'expert', 'dp')), may hold values from 0 to 15, all different within a row; in each aligned block of 8 rows (0 to 7, 8 to 15, ...) at most 5 rows name the same one
- replica_choice: int32 [256, 8], P(('groups', 'expert', 'dp')), may hold values from 0 to 3
- replica_cols: int32 [2, 4], replicated, may hold values from 0 to 7, as said below
- combine_weight: float32 [256, 8], P(('groups', 'expert', 'dp')), may hold values from 0.1 to 0.5
Outputs:
- mixed: bfloat16 [256, 4096], P(('groups', 'expert', 'dp'))
- loads: float32 [32, 2], P(('groups', 'expert', 'dp'))
The draws below stay inside these ranges and needn't reach their ends.
Inputs may be any that keep to these rules, and one draw needn't show every extreme that they name: `experts_chosen`: in each device's 8 tokens no expert is named more than 5 times; a token names 8 different experts. `replica_cols`: each row names 4 different columns of the expert axis.
All inputs are finite; a program needn't handle non-finite values.
Results may differ from the reference program's by a relative error of at most 0.0072.
Values may be sent and summed in bfloat16 or wider, within the bound.
A program may use at most 64 MiB of HBM per device.

```python
import math
import jax
import jax.numpy as jnp
import numpy as np
from jax import lax

D = 4096
FF = 768
TOP = 8
REPS = 4
TOK_DEV = 8
PIECES = 32
EXPERTS = 16
PIECE_FF = 384
PAIRS_COL = 2
TOKENS = 256
MOST = 5
N_EXPERT = 8
N_DP = 4


def draw_replica_cols(key, part):
    key = jax.random.fold_in(key, 7)
    row_keys = jax.random.split(key, PAIRS_COL)

    def one_row(row_key):
        return jax.random.permutation(row_key, N_EXPERT)[:REPS]
    return jax.vmap(one_row)(row_keys).astype(jnp.int32)


def touch_ends(entries, rng, least, high):
    spot = [jax.random.randint(jax.random.fold_in(rng, axis), (), 0, length) for axis, length in enumerate(entries.shape)]
    widest = entries.shape.index(max(entries.shape))
    next_to = spot[:widest] + [(spot[widest] + 1) % entries.shape[widest]] + spot[widest + 1:]
    return entries.at[tuple(spot)].set(least).at[tuple(next_to)].set(high)


def block_levels(key, dims, shards, smallest, high):
    loudness, own = 1.0, jax.random.fold_in(key, 6)
    for dim, blocks in shards:
        steps = jnp.exp(jax.random.uniform(jax.random.fold_in(own, dim), (blocks,), jnp.float32, smallest / len(shards), high / len(shards)))
        loudness = loudness * jnp.repeat(steps, dims[dim] // blocks).reshape([-1 if axis == dim else 1 for axis in range(len(dims))])
    return loudness


def routed_block(own_key, own, number, rows, count, top, reach, lean):
    sequence = jax.random.permutation(own_key, count)
    packed, common = portions_of(count, rows * top, reach, lean, True), portions_of(count, rows * top, reach, lean, False)
    places = jnp.arange(count)

    def named(sizes, rotation):
        used = int((sizes > 0).sum())
        fixed = max(1, used // 4)
        shifted = fixed + (places - fixed + rotation * (used - fixed)) % max(1, count - fixed)
        return jnp.zeros((count,), jnp.int32).at[sequence[jnp.where(places < fixed, places, shifted)]].set(jnp.asarray(sizes, jnp.int32))

    sizes = jnp.where(number % 4 == 0, named(packed, number // 4), named(common, number - number // 4 - 1))
    mixed = jax.random.permutation(jax.random.fold_in(own, 3), count)
    donor, taker = mixed[0:count // 2 * 2:2], mixed[1:count // 2 * 2:2]
    margin = jnp.minimum(sizes[donor] - 1, reach - sizes[taker]) // 2
    margin = jnp.where((donor == sequence[0]) | (taker == sequence[0]) | (sizes[taker] == 0), 0, jnp.maximum(margin, 0))
    shifted = jax.random.randint(jax.random.fold_in(own, 4), (count // 2,), 0, 1 << 20) % (margin + 1)
    sizes = sizes.at[donor].add(-shifted).at[taker].add(shifted)
    items = jnp.searchsorted(jnp.cumsum(sizes), jnp.arange(rows * top), side="right").astype(jnp.int32)
    table = items.reshape(top, rows).T
    table = table[jax.random.permutation(jax.random.fold_in(own, 1), rows)]
    rotation = jax.random.randint(jax.random.fold_in(own, 2), (rows, 1), 0, top)
    return jnp.take_along_axis(table, (jnp.arange(top)[None, :] + rotation) % top, axis=1)


def portions_of(count, total, reach, skew, full):
    weights = [(1 << 20) // math.isqrt(grade ** skew) + 1 for grade in range(1, count + 1)]
    largest = reach if full else min(reach, max(-(-total // count), total * weights[0] // sum(weights)))
    least = 1 if total - largest >= count - 1 else 0
    given, surplus = [largest] + [least] * (count - 1), total - largest - least * (count - 1)
    while surplus > 0:
        free = [i for i in range(1, count) if given[i] < largest] or [i for i in range(1, count) if given[i] < reach]
        mass, remaining = sum([weights[i] for i in free]), surplus
        for i in free:
            extra = min(reach - given[i], max(1, remaining * weights[i] // mass), surplus)
            given[i] = given[i] + extra
            surplus = surplus - extra
    return np.array(given)


def centred(rng, shape, spread, limit, cuts=(), held_as=jnp.bfloat16):
    result = jax.random.normal(rng, shape, jnp.float32) * spread
    if len(cuts) > 0:
        result = block_levels(rng, shape, cuts, -0.22, 0.18) * result
    return jnp.clip(result, min=-limit, max=limit).astype(held_as)


def setup_inputs(seed: int = 0, part: int = 0) -> dict:
    arg_keys = jax.random.split(jax.random.key(seed), 10)
    own_keys = jax.random.split(jax.random.fold_in(arg_keys[9], part), 10)
    tokens = centred(own_keys[0], (TOKENS, D), 1.0, 6.0, ((0, 32),))
    norm_gain = jnp.clip(1.0 + 0.18 * jax.random.normal(arg_keys[1], (D,), jnp.float32), 0.1, 1.9)
    gate_weight = centred(arg_keys[2], (PIECES, D, PIECE_FF), D ** -0.5, 0.09375, ((0, 32),))
    up_weight = centred(arg_keys[3], (PIECES, D, PIECE_FF), D ** -0.5, 0.09375, ((0, 32),))
    down_weight = centred(arg_keys[4], (PIECES, PIECE_FF, D), FF ** -0.5, 0.21875, ((0, 32),))
    experts_chosen_keys = jax.random.split(jax.random.fold_in(own_keys[5], 1), TOKENS // TOK_DEV)
    experts_chosen_turns = jax.random.permutation(jax.random.fold_in(own_keys[5], 3), TOKENS // TOK_DEV)
    experts_chosen = jax.vmap(lambda own, number: routed_block(jax.random.fold_in(own_keys[5], 2), own, number, TOK_DEV, EXPERTS, TOP, MOST, 2))(experts_chosen_keys, experts_chosen_turns).reshape((TOKENS, TOP))
    replica_choice = touch_ends(jax.random.randint(own_keys[6], (TOKENS, TOP), 0, REPS), jax.random.fold_in(own_keys[6], 1), 0, REPS - 1).astype(jnp.int32)
    replica_cols = draw_replica_cols(jax.random.fold_in(arg_keys[9], 71), part)
    combine_weight = jnp.clip(jnp.exp(math.log(0.5) - 1.609438 * jax.random.uniform(own_keys[8], (TOKENS, TOP), jnp.float32) ** block_levels(own_keys[8], (TOKENS, TOP), ((0, 32),), -0.2, 0.2)), 0.1, 0.5)
    return dict(tokens=tokens, norm_gain=norm_gain, gate_weight=gate_weight, up_weight=up_weight, down_weight=down_weight, experts_chosen=experts_chosen, replica_choice=replica_choice, replica_cols=replica_cols, combine_weight=combine_weight)


def holders(experts_chosen, replica_choice, replica_cols, pair_cols):
    column = experts_chosen // pair_cols
    within = experts_chosen % pair_cols
    home_col = replica_cols[within, 0]
    chosen_col = replica_cols[within, replica_choice]
    holder_col = jnp.where(column == home_col, chosen_col, column)
    slot_index = (holder_col != column).astype(jnp.int32)
    return (holder_col * pair_cols + within, slot_index)

def reference(tokens, norm_gain, gate_weight, up_weight, down_weight, experts_chosen, replica_choice, replica_cols, combine_weight):
    values = tokens.astype(jnp.float32)
    scale = lax.rsqrt(lax.optimization_barrier(jnp.mean(values * values, axis=1, keepdims=True)) + 1e-06)
    normed = (values * scale * norm_gain).astype(jnp.bfloat16)
    capacity = MOST * N_EXPERT * N_DP

    def one_expert(summed, expert_id):
        named_here = experts_chosen == expert_id
        chosen = jnp.any(named_here, axis=1)
        row_ids = jnp.nonzero(chosen, size=capacity, fill_value=0)[0].astype(jnp.int32)
        in_use = jnp.arange(capacity) < jnp.sum(chosen.astype(jnp.int32))
        slot_rows = normed[row_ids]
        weight = lax.optimization_barrier(jnp.sum(jnp.where(named_here, combine_weight, jnp.zeros_like(combine_weight)), axis=1))[row_ids]
        weight = jnp.where(in_use, weight, jnp.zeros_like(weight))
        result_rows = jnp.zeros((capacity, D), jnp.float32)
        for half_index in range(2):
            piece_index = 2 * expert_id + half_index
            gate_out = jnp.dot(slot_rows, gate_weight[piece_index], preferred_element_type=jnp.float32)
            up_out = jnp.dot(slot_rows, up_weight[piece_index], preferred_element_type=jnp.float32)
            hidden = (jax.nn.silu(gate_out) * up_out).astype(jnp.bfloat16)
            piece_out = jnp.dot(hidden, down_weight[piece_index], preferred_element_type=jnp.float32).astype(jnp.bfloat16)
            result_rows = result_rows + piece_out.astype(jnp.float32)
        summed = summed.at[row_ids].add(weight[:, None] * result_rows)
        return (summed, None)
    summed, _ = lax.scan(one_expert, jnp.zeros((TOKENS, D), jnp.float32), jnp.arange(EXPERTS, dtype=jnp.int32))
    mixed = summed.astype(jnp.bfloat16)
    holder_pair, slot_index = holders(experts_chosen, replica_choice, replica_cols, PAIRS_COL)
    plan_key = (holder_pair * 2 + slot_index).reshape(-1)
    key_counts = lax.optimization_barrier(jnp.sum((plan_key[:, None] == jnp.arange(N_EXPERT * N_DP, dtype=jnp.int32)[None, :]).astype(jnp.float32), axis=0))
    loads = jnp.repeat(key_counts.reshape(-1, 2), 2, axis=0) / jnp.float32(TOK_DEV)
    return (mixed, loads)
```

```python
import jax
import jax.numpy as jnp
from jax import lax
from jax.sharding import PartitionSpec as P


def plan(experts_chosen, replica_choice, replica_cols, combine_weight, pair_cols, pair_count):
    rep_count = replica_cols.shape[1]
    column = experts_chosen // pair_cols
    within = experts_chosen % pair_cols
    rows_hot = within[..., None] == jnp.arange(pair_cols, dtype=jnp.int32)
    home_col = jnp.sum(jnp.where(rows_hot, replica_cols[:, 0], 0), axis=-1)
    flat_hot = (within * rep_count + replica_choice)[..., None] == jnp.arange(
        pair_cols * rep_count, dtype=jnp.int32
    )
    chosen_col = jnp.sum(jnp.where(flat_hot, replica_cols.reshape(-1), 0), axis=-1)
    holder_col = jnp.where(column == home_col, chosen_col, column)
    plan_slot = (holder_col != column).astype(jnp.int32)
    plan_key = (holder_col * pair_cols + within) * 2 + plan_slot
    keys = jnp.arange(pair_count * 2, dtype=jnp.int32)
    counts = jnp.sum((plan_key[..., None] == keys).astype(jnp.float32), axis=1)
    experts = jnp.arange(pair_count, dtype=jnp.int32)
    weights = jnp.sum(
        jnp.where(experts_chosen[..., None] == experts, combine_weight[..., None], 0.0), axis=1
    )
    return counts, weights


def per_device(
    tokens,
    norm_gain,
    gate_weight,
    up_weight,
    down_weight,
    experts_chosen,
    replica_choice,
    replica_cols,
    combine_weight,
):
    expert_count = lax.axis_size("expert")
    dp_count = lax.axis_size("dp")
    axes = ("expert", "dp")
    pair_cols = dp_count // 2
    pair_count = expert_count * pair_cols
    tok_rows = tokens.shape[0]
    values = tokens.astype(jnp.float32)
    scale = lax.rsqrt(jnp.mean(values * values, axis=1, keepdims=True) + 1e-06)
    normed = (values * scale * norm_gain).astype(jnp.bfloat16)
    counts, weights = plan(
        experts_chosen, replica_choice, replica_cols, combine_weight, pair_cols, pair_count
    )
    side = jnp.concatenate([weights, counts], axis=1)
    side = lax.all_gather(side, axes, axis=0, tiled=True)
    rows = lax.all_gather(normed, axes, axis=0, tiled=True)
    pair = lax.axis_index("expert") * pair_cols + lax.axis_index("dp") // 2
    weight = lax.dynamic_slice_in_dim(side, pair, 1, axis=1)
    served = jnp.sum(lax.dynamic_slice_in_dim(side, pair_count + 2 * pair, 2, axis=1), axis=0)
    loads = (served / jnp.float32(tok_rows))[None, :]
    gate_out = jnp.dot(rows, gate_weight[0], preferred_element_type=jnp.float32)
    up_out = jnp.dot(rows, up_weight[0], preferred_element_type=jnp.float32)
    hidden = (jax.nn.silu(gate_out) * up_out).astype(jnp.bfloat16)
    out = jnp.dot(hidden, down_weight[0], preferred_element_type=jnp.float32) * weight
    mixed = lax.psum_scatter(out, axes, scatter_dimension=0, tiled=True).astype(jnp.bfloat16)
    return (mixed, loads)


def solution(mesh):
    rows = P(("groups", "expert", "dp"), None)
    pieces = P(("expert", "dp"), None, None)
    return jax.shard_map(
        per_device,
        mesh=mesh,
        in_specs=(rows, P(), pieces, pieces, pieces, rows, rows, P(), rows),
        out_specs=(rows, rows),
        check_vma=False,
    )
```

```python
import functools

import jax
import jax.numpy as jnp
from jax import lax
from jax.experimental import pallas as pl
from jax.experimental.pallas import tpu as pltpu
from jax.sharding import PartitionSpec as P

MESH = pl.DeviceIdType.MESH
LANES = 128
BF16 = jnp.bfloat16
F32 = jnp.float32


def plan(experts_chosen, replica_choice, replica_cols, combine_weight, pair_cols, pair_count):
    rep_count = replica_cols.shape[1]
    column = experts_chosen // pair_cols
    within = experts_chosen % pair_cols
    rows_hot = within[..., None] == jnp.arange(pair_cols, dtype=jnp.int32)
    home_col = jnp.sum(jnp.where(rows_hot, replica_cols[:, 0], 0), axis=-1)
    flat_hot = (within * rep_count + replica_choice)[..., None] == jnp.arange(
        pair_cols * rep_count, dtype=jnp.int32
    )
    chosen_col = jnp.sum(jnp.where(flat_hot, replica_cols.reshape(-1), 0), axis=-1)
    holder_col = jnp.where(column == home_col, chosen_col, column)
    plan_slot = (holder_col != column).astype(jnp.int32)
    plan_key = (holder_col * pair_cols + within) * 2 + plan_slot
    keys = jnp.arange(pair_count * 2, dtype=jnp.int32)
    counts = jnp.sum((plan_key[..., None] == keys).astype(jnp.float32), axis=1)
    experts = jnp.arange(pair_count, dtype=jnp.int32)
    weights = jnp.sum(
        jnp.where(experts_chosen[..., None] == experts, combine_weight[..., None], 0.0), axis=1
    )
    return counts, weights


def fused_kernel(
    depth, rep_count, tokens_ref, gain_ref, chosen_ref, choice_ref, cols_ref, combine_ref,
    gate_hbm, up_hbm, down_hbm, mixed_ref, loads_ref,
    gate_v, up_v, down_v, swap_out, swap_in, g0, g1, gate_acc, up_acc, hidden_v,
    s1, r1, own, s2, r2, s3, r3, f_out, f_in,
    load_sem, pair_send, pair_recv, z_send, z_recv, a1_send, a1_recv, a2_send, a2_recv,
    sib_send, sib_recv, c1_send, c1_recv, c2_send, c2_recv, c3_send, c3_recv,
):
    grow = (g0, g1)
    tok_rows, width = tokens_ref.shape
    half, quarter = width // 2, width // 4
    ff = gate_v.shape[1]
    experts = depth * 4
    expert, dp = lax.axis_index("expert"), lax.axis_index("dp")
    z, y, x, c = expert // 2, expert % 2, dp // 2, dp % 2
    chip = expert * 2 + x
    here = y * 2 + x
    cat = (here, y * 2 + 1 - x, (1 - y) * 2 + x, (1 - y) * 2 + 1 - x)
    sibling = {"expert": expert, "dp": x * 2 + 1 - c}
    x_next = {"expert": expert, "dp": (1 - x) * 2 + c}
    y_next = {"expert": z * 2 + 1 - y, "dp": dp}
    near = (x_next, y_next)

    def z_at(step):
        return {"expert": lax.rem(z + step, depth) * 2 + y, "dp": dp}

    sends = []

    def send(src, dst, send_sem, recv_sem, device):
        copy = pltpu.make_async_remote_copy(
            src_ref=src, dst_ref=dst, send_sem=send_sem, recv_sem=recv_sem,
            device_id=device, device_id_type=MESH,
        )
        copy.start()
        sends.append(copy)

    def arrived(ref, send_sem, recv_sem):
        pltpu.make_async_remote_copy(
            src_ref=ref, dst_ref=ref, send_sem=send_sem, recv_sem=recv_sem,
            device_id=sibling, device_id_type=MESH,
        ).wait_recv()

    loads_in = [
        pltpu.make_async_copy(gate_hbm.at[0], gate_v, load_sem.at[0]),
        pltpu.make_async_copy(up_hbm.at[0], up_v, load_sem.at[1]),
        pltpu.make_async_copy(
            down_hbm.at[0, :, pl.ds(pl.multiple_of(c * half, half), half)],
            down_v.at[c], load_sem.at[2],
        ),
    ]
    for copy in loads_in:
        copy.start()

    barrier = pltpu.get_barrier_semaphore()
    partners = [sibling, x_next, y_next] + [z_at(step) for step in range(1, depth)]
    for partner in partners:
        pl.semaphore_signal(barrier, inc=1, device_id=partner, device_id_type=MESH)

    values = tokens_ref[...].astype(F32)
    scale = lax.rsqrt(jnp.mean(values * values, axis=1, keepdims=True) + 1e-06)
    normed = (values * scale * gain_ref[...]).astype(BF16).astype(F32)
    lane = lax.broadcasted_iota(jnp.int32, (tok_rows, LANES), 1)
    side = jnp.zeros((tok_rows, LANES), F32)
    for k in range(chosen_ref.shape[1]):
        name = chosen_ref[:, k : k + 1]
        pick = choice_ref[:, k : k + 1]
        odd = (name & 1) == 1
        home = jnp.where(odd, cols_ref[1, 0], cols_ref[0, 0])
        holder = jnp.zeros_like(name)
        for r in range(rep_count):
            holder = jnp.where(pick == r, jnp.where(odd, cols_ref[1, r], cols_ref[0, r]), holder)
        column = name >> 1
        holder = jnp.where(column == home, holder, column)
        slot = jnp.where(holder == column, 0, 1)
        key = (holder * 2 + (name & 1)) * 2 + slot
        weight = combine_ref[:, k : k + 1]
        named = (lane == name) | (lane == name + experts)
        side = side + jnp.where(named, weight, 0.0)
        side = side + jnp.where(lane == key + 2 * experts, 1.0, 0.0)
    left, right = normed[:, :half], normed[:, half:]
    mine = jnp.where(c == 0, left, right)
    swap_out[:, :half] = jnp.where(c == 0, right, left)
    swap_out[:, half:] = side

    pl.semaphore_wait(barrier, len(partners))
    send(swap_out, swap_in, pair_send.at[0], pair_recv.at[0], sibling)
    send(
        down_hbm.at[0, :, pl.ds(pl.multiple_of((1 - c) * half, half), half)],
        down_v.at[c], pair_send.at[1], pair_recv.at[1], sibling,
    )
    arrived(swap_in, pair_send.at[0], pair_recv.at[0])
    other = swap_in[:, :half]
    rows = jnp.concatenate(
        [jnp.where(c == 0, mine, other), jnp.where(c == 0, other, mine)], axis=0
    ).astype(BF16)
    other_side = swap_in[:, half:]
    side = jnp.concatenate(
        [jnp.where(c == 0, side, other_side), jnp.where(c == 0, other_side, side)], axis=0
    )
    lanes = lax.broadcasted_iota(jnp.int32, side.shape, 1)
    low = (lanes >= experts) & (lanes < 2 * experts)
    side = jnp.where(low, side - side.astype(BF16).astype(F32), side).astype(BF16)
    g0[c, here, z, :, :quarter] = rows[:, :quarter]
    g0[c, here, z, :, quarter:] = side
    g1[c, here, z] = rows[:, quarter:]

    def block(q, place, step):
        return grow[q].at[c, place, lax.rem(z - step + depth, depth)]

    def to_sibling(q, kind, step):
        ref = block(q, cat[kind], step)
        send(ref, ref, sib_send.at[q, kind, step], sib_recv.at[q, kind, step], sibling)

    def spread(step):
        for q in range(2):
            ref = block(q, here, step)
            send(ref, ref, a1_send.at[q, step], a1_recv.at[q, step], near[q])
        for q in range(2):
            ref = block(q, here, step)
            send(ref, ref, a2_send.at[q, 0, step], a2_recv.at[q, 0, step], near[1 - q])
            to_sibling(q, 0, step)

    def forward(step):
        for q in range(2):
            ref = block(q, cat[1 + q], step)
            arrived(ref, a1_send.at[q, step], a1_recv.at[q, step])
            send(ref, ref, a2_send.at[q, 1, step], a2_recv.at[q, 1, step], near[1 - q])
            to_sibling(q, 1 + q, step)

    for step in range(1, depth):
        for q in range(2):
            ref = block(q, here, 0)
            send(ref, ref, z_send.at[q, step], z_recv.at[q, step], z_at(step))
    spread(0)
    for step in range(1, depth):
        for q in range(2):
            arrived(block(q, here, step), z_send.at[q, step], z_recv.at[q, step])
        spread(step)
        forward(step - 1)
    forward(depth - 1)
    for step in range(depth):
        for q in range(2):
            for j in range(2):
                kind = 3 if j == 1 else 2 - q
                arrived(block(q, cat[kind], step), a2_send.at[q, j, step], a2_recv.at[q, j, step])
                to_sibling(q, kind, step)

    all_rows = 4 * depth * 2 * tok_rows
    for copy in loads_in:
        copy.wait()

    def project(h, first):
        for q in range(2):
            block_rows = grow[q][h, :, :, :, :quarter].reshape(all_rows, quarter)
            at = pl.ds(pl.multiple_of(h * half + q * quarter, quarter), quarter)
            gate = jnp.dot(block_rows, gate_v[at, :], preferred_element_type=F32)
            up = jnp.dot(block_rows, up_v[at, :], preferred_element_type=F32)
            if first and q == 0:
                gate_acc[...] = gate
                up_acc[...] = up
            else:
                gate_acc[...] += gate
                up_acc[...] += up

    project(c, True)
    for step in range(depth):
        for q in range(2):
            for kind in range(4):
                ref = grow[q].at[1 - c, cat[kind], lax.rem(z - step + depth, depth)]
                arrived(ref, sib_send.at[q, kind, step], sib_recv.at[q, kind, step])
    project(1 - c, False)
    gate = gate_acc[...]
    hidden = gate * (1.0 / (1.0 + jnp.exp(-gate))) * up_acc[...]
    hidden_v[c] = hidden.astype(BF16)
    send(hidden_v.at[c], hidden_v.at[c], pair_send.at[2], pair_recv.at[2], sibling)

    meta = g0[c, :, :, :, quarter:].reshape(all_rows, LANES).astype(F32)
    meta_lane = lax.broadcasted_iota(jnp.int32, meta.shape, 1)
    ours = (meta_lane == chip) | (meta_lane == chip + experts)
    weights = jnp.sum(jnp.where(ours, meta, 0.0), axis=1, keepdims=True)
    gate_acc[:, :LANES] = jnp.broadcast_to(weights, (all_rows, LANES))
    totals = jnp.sum(meta, axis=0, keepdims=True)
    total_lane = lax.broadcasted_iota(jnp.int32, totals.shape, 1)
    base = 2 * experts + 2 * chip
    home_count = jnp.sum(jnp.where(total_lane == base, totals, 0.0), axis=1, keepdims=True)
    copy_count = jnp.sum(jnp.where(total_lane == base + 1, totals, 0.0), axis=1, keepdims=True)
    two = lax.broadcasted_iota(jnp.int32, (1, 2), 1)
    loads_ref[...] = jnp.where(two == 0, home_count, copy_count) / tok_rows

    arrived(down_v.at[1 - c], pair_send.at[1], pair_recv.at[1])
    arrived(hidden_v.at[1 - c], pair_send.at[2], pair_recv.at[2])
    line = depth * 2 * tok_rows

    def line_rows(ref, place):
        return ref[pl.ds(pl.multiple_of(place * line, line), line), :]

    def outputs(q, places):
        total = None
        for p in range(2):
            part = jnp.concatenate([line_rows(hidden_v.at[p], place) for place in places], axis=0)
            at = slice(q * quarter, (q + 1) * quarter)
            term = jnp.dot(part, down_v[p, :, at], preferred_element_type=F32)
            total = term if total is None else total + term
        factor = jnp.concatenate(
            [line_rows(gate_acc, place)[:, :1] for place in places], axis=0
        )
        return (total * factor).reshape(2, depth, 2 * tok_rows, quarter)

    back = (y_next, x_next)
    order = list(range(1, depth)) + [0]
    for q in range(2):
        far = (cat[3], cat[2 - q])
        s1[q] = outputs(q, far).astype(BF16)
        for j in range(2):
            for step in order:
                to = lax.rem(z + step, depth)
                send(
                    s1.at[q, j, to], r1.at[q, j, to],
                    c1_send.at[q, j, step], c1_recv.at[q, j, step], back[q],
                )
    for q in range(2):
        own[q] = outputs(q, (cat[1 + q], here))
    for step in order:
        for q in range(2):
            to = lax.rem(z + step, depth)
            arrived(r1.at[q, 0, to], c1_send.at[q, 0, step], c1_recv.at[q, 0, step])
            s2[q, to] = (own[q, 0, to] + r1[q, 0, to].astype(F32)).astype(BF16)
            send(
                s2.at[q, to], r2.at[q, to],
                c2_send.at[q, step], c2_recv.at[q, step], back[1 - q],
            )
    for step in order:
        for q in range(2):
            to = lax.rem(z + step, depth)
            arrived(r1.at[q, 1, to], c1_send.at[q, 1, step], c1_recv.at[q, 1, step])
            arrived(r2.at[q, to], c2_send.at[q, step], c2_recv.at[q, step])
            value = own[q, 1, to] + r1[q, 1, to].astype(F32) + r2[q, to].astype(F32)
            if step == 0:
                own[q, 1, to] = value
            else:
                s3[q, step] = value.astype(BF16)
                send(
                    s3.at[q, step], r3.at[q, step],
                    c3_send.at[q, step], c3_recv.at[q, step], z_at(step),
                )
    kept = []
    for q in range(2):
        value = own[q, 1, z]
        for step in range(1, depth):
            arrived(r3.at[q, step], c3_send.at[q, step], c3_recv.at[q, step])
            value = value + r3[q, step].astype(F32)
        top, bottom = value[:tok_rows], value[tok_rows:]
        f_out[q] = jnp.where(c == 0, bottom, top)
        kept.append(jnp.where(c == 0, top, bottom))
    send(f_out, f_in, pair_send.at[3], pair_recv.at[3], sibling)
    arrived(f_in, pair_send.at[3], pair_recv.at[3])
    for q in range(2):
        there = f_in[q]
        for h in range(2):
            mixed_ref[:, h * half + q * quarter : h * half + (q + 1) * quarter] = jnp.where(
                c == h, kept[q], there
            ).astype(BF16)
    for copy in sends:
        copy.wait_send()


def fused(tokens, norm_gain, gate, up, down, chosen, choice, cols, combine):
    tok_rows, width = tokens.shape
    ff = gate.shape[2]
    depth = lax.axis_size("expert") // 2
    half, quarter, pair_rows = width // 2, width // 4, 2 * tok_rows
    rows = 4 * depth * pair_rows
    vmem = pl.BlockSpec(memory_space=pltpu.VMEM)
    smem = pl.BlockSpec(memory_space=pltpu.SMEM)
    anywhere = pl.BlockSpec(memory_space=pl.ANY)
    dma = pltpu.SemaphoreType.DMA
    return pl.pallas_call(
        functools.partial(fused_kernel, depth, cols.shape[1]),
        out_shape=(
            jax.ShapeDtypeStruct((tok_rows, width), BF16),
            jax.ShapeDtypeStruct((1, 2), F32),
        ),
        in_specs=[vmem, vmem, vmem, vmem, smem, vmem, anywhere, anywhere, anywhere],
        out_specs=(vmem, vmem),
        scratch_shapes=[
            pltpu.VMEM((width, ff), BF16),
            pltpu.VMEM((width, ff), BF16),
            pltpu.VMEM((2, ff, half), BF16),
            pltpu.VMEM((tok_rows, half + LANES), F32),
            pltpu.VMEM((tok_rows, half + LANES), F32),
            pltpu.VMEM((2, 4, depth, pair_rows, quarter + LANES), BF16),
            pltpu.VMEM((2, 4, depth, pair_rows, quarter), BF16),
            pltpu.VMEM((rows, ff), F32),
            pltpu.VMEM((rows, ff), F32),
            pltpu.VMEM((2, rows, ff), BF16),
            pltpu.VMEM((2, 2, depth, pair_rows, quarter), BF16),
            pltpu.VMEM((2, 2, depth, pair_rows, quarter), BF16),
            pltpu.VMEM((2, 2, depth, pair_rows, quarter), F32),
            pltpu.VMEM((2, depth, pair_rows, quarter), BF16),
            pltpu.VMEM((2, depth, pair_rows, quarter), BF16),
            pltpu.VMEM((2, depth, pair_rows, quarter), BF16),
            pltpu.VMEM((2, depth, pair_rows, quarter), BF16),
            pltpu.VMEM((2, tok_rows, quarter), F32),
            pltpu.VMEM((2, tok_rows, quarter), F32),
            dma((3,)), dma((4,)), dma((4,)),
            dma((2, depth)), dma((2, depth)), dma((2, depth)), dma((2, depth)),
            dma((2, 2, depth)), dma((2, 2, depth)), dma((2, 4, depth)), dma((2, 4, depth)),
            dma((2, 2, depth)), dma((2, 2, depth)), dma((2, depth)), dma((2, depth)),
            dma((2, depth)), dma((2, depth)),
        ],
        compiler_params=pltpu.CompilerParams(
            collective_id=0, has_side_effects=True, vmem_limit_bytes=56 * 1024 * 1024
        ),
    )(tokens, norm_gain.reshape(1, width), chosen, choice, cols, combine, gate, up, down)


def per_device(
    tokens,
    norm_gain,
    gate_weight,
    up_weight,
    down_weight,
    experts_chosen,
    replica_choice,
    replica_cols,
    combine_weight,
):
    expert_count = lax.axis_size("expert")
    dp_count = lax.axis_size("dp")
    axes = ("expert", "dp")
    if dp_count == 4 and expert_count % 2 == 0 and expert_count * 8 <= LANES:
        return fused(
            tokens, norm_gain, gate_weight, up_weight, down_weight,
            experts_chosen, replica_choice, replica_cols, combine_weight,
        )
    pair_cols = dp_count // 2
    pair_count = expert_count * pair_cols
    tok_rows = tokens.shape[0]
    values = tokens.astype(jnp.float32)
    scale = lax.rsqrt(jnp.mean(values * values, axis=1, keepdims=True) + 1e-06)
    normed = (values * scale * norm_gain).astype(jnp.bfloat16)
    counts, weights = plan(
        experts_chosen, replica_choice, replica_cols, combine_weight, pair_cols, pair_count
    )
    side = jnp.concatenate([weights, counts], axis=1)
    side = lax.all_gather(side, axes, axis=0, tiled=True)
    rows = lax.all_gather(normed, axes, axis=0, tiled=True)
    pair = lax.axis_index("expert") * pair_cols + lax.axis_index("dp") // 2
    weight = lax.dynamic_slice_in_dim(side, pair, 1, axis=1)
    served = jnp.sum(lax.dynamic_slice_in_dim(side, pair_count + 2 * pair, 2, axis=1), axis=0)
    loads = (served / jnp.float32(tok_rows))[None, :]
    gate_out = jnp.dot(rows, gate_weight[0], preferred_element_type=jnp.float32)
    up_out = jnp.dot(rows, up_weight[0], preferred_element_type=jnp.float32)
    hidden = (jax.nn.silu(gate_out) * up_out).astype(jnp.bfloat16)
    out = jnp.dot(hidden, down_weight[0], preferred_element_type=jnp.float32) * weight
    mixed = lax.psum_scatter(out, axes, scatter_dimension=0, tiled=True).astype(jnp.bfloat16)
    return (mixed, loads)


def solution(mesh):
    rows = P(("groups", "expert", "dp"), None)
    pieces = P(("expert", "dp"), None, None)
    return jax.shard_map(
        per_device,
        mesh=mesh,
        in_specs=(rows, P(), pieces, pieces, pieces, rows, rows, P(), rows),
        out_specs=(rows, rows),
        check_vma=False,
    )
```

```python
import functools

import jax
import jax.numpy as jnp
from jax import lax
from jax.experimental import pallas as pl
from jax.experimental.pallas import tpu as pltpu
from jax.sharding import PartitionSpec as P

MESH = pl.DeviceIdType.MESH
LANES = 128
BF16 = jnp.bfloat16
F32 = jnp.float32


def plan(experts_chosen, replica_choice, replica_cols, combine_weight, pair_cols, pair_count):
    rep_count = replica_cols.shape[1]
    column = experts_chosen // pair_cols
    within = experts_chosen % pair_cols
    rows_hot = within[..., None] == jnp.arange(pair_cols, dtype=jnp.int32)
    home_col = jnp.sum(jnp.where(rows_hot, replica_cols[:, 0], 0), axis=-1)
    flat_hot = (within * rep_count + replica_choice)[..., None] == jnp.arange(
        pair_cols * rep_count, dtype=jnp.int32
    )
    chosen_col = jnp.sum(jnp.where(flat_hot, replica_cols.reshape(-1), 0), axis=-1)
    holder_col = jnp.where(column == home_col, chosen_col, column)
    plan_slot = (holder_col != column).astype(jnp.int32)
    plan_key = (holder_col * pair_cols + within) * 2 + plan_slot
    keys = jnp.arange(pair_count * 2, dtype=jnp.int32)
    counts = jnp.sum((plan_key[..., None] == keys).astype(jnp.float32), axis=1)
    experts = jnp.arange(pair_count, dtype=jnp.int32)
    weights = jnp.sum(
        jnp.where(experts_chosen[..., None] == experts, combine_weight[..., None], 0.0), axis=1
    )
    return counts, weights


def fused_kernel(
    depth, rep_count, tokens_ref, gain_ref, chosen_ref, choice_ref, cols_ref, combine_ref,
    gate_hbm, up_hbm, down_hbm, mixed_ref, loads_ref,
    gate_v, up_v, down_v, swap_out, swap_in, g0, g1, gate_acc, up_acc, hidden_v,
    s1, r1, own, s2, r2, s3, r3, f_out, f_in,
    load_sem, pair_send, pair_recv, z_send, z_recv, a1_send, a1_recv, a2_send, a2_recv,
    sib_send, sib_recv, c1_send, c1_recv, c2_send, c2_recv, c3_send, c3_recv,
):
    grow = (g0, g1)
    tok_rows, width = tokens_ref.shape
    half, quarter = width // 2, width // 4
    ff = gate_v.shape[1]
    experts = depth * 4
    expert, dp = lax.axis_index("expert"), lax.axis_index("dp")
    z, y, x, c = expert // 2, expert % 2, dp // 2, dp % 2
    chip = expert * 2 + x
    here = y * 2 + x
    cat = (here, y * 2 + 1 - x, (1 - y) * 2 + x, (1 - y) * 2 + 1 - x)
    sibling = {"expert": expert, "dp": x * 2 + 1 - c}
    x_next = {"expert": expert, "dp": (1 - x) * 2 + c}
    y_next = {"expert": z * 2 + 1 - y, "dp": dp}
    near = (x_next, y_next)

    def z_at(step):
        return {"expert": lax.rem(z + step, depth) * 2 + y, "dp": dp}

    sends = []

    def send(src, dst, send_sem, recv_sem, device):
        copy = pltpu.make_async_remote_copy(
            src_ref=src, dst_ref=dst, send_sem=send_sem, recv_sem=recv_sem,
            device_id=device, device_id_type=MESH,
        )
        copy.start()
        sends.append(copy)

    def arrived(ref, send_sem, recv_sem):
        pltpu.make_async_remote_copy(
            src_ref=ref, dst_ref=ref, send_sem=send_sem, recv_sem=recv_sem,
            device_id=sibling, device_id_type=MESH,
        ).wait_recv()

    loads_in = [
        pltpu.make_async_copy(gate_hbm.at[0], gate_v, load_sem.at[0]),
        pltpu.make_async_copy(up_hbm.at[0], up_v, load_sem.at[1]),
        pltpu.make_async_copy(
            down_hbm.at[0, :, pl.ds(pl.multiple_of(c * half, half), half)],
            down_v.at[c], load_sem.at[2],
        ),
    ]
    for copy in loads_in:
        copy.start()

    barrier = pltpu.get_barrier_semaphore()
    partners = [sibling, x_next, y_next] + [z_at(step) for step in range(1, depth)]
    for partner in partners:
        pl.semaphore_signal(barrier, inc=1, device_id=partner, device_id_type=MESH)

    values = tokens_ref[...].astype(F32)
    scale = lax.rsqrt(jnp.mean(values * values, axis=1, keepdims=True) + 1e-06)
    normed = (values * scale * gain_ref[...]).astype(BF16).astype(F32)
    lane = lax.broadcasted_iota(jnp.int32, (tok_rows, LANES), 1)
    side = jnp.zeros((tok_rows, LANES), F32)
    for k in range(chosen_ref.shape[1]):
        name = chosen_ref[:, k : k + 1]
        pick = choice_ref[:, k : k + 1]
        odd = (name & 1) == 1
        home = jnp.where(odd, cols_ref[1, 0], cols_ref[0, 0])
        holder = jnp.zeros_like(name)
        for r in range(rep_count):
            holder = jnp.where(pick == r, jnp.where(odd, cols_ref[1, r], cols_ref[0, r]), holder)
        column = name >> 1
        holder = jnp.where(column == home, holder, column)
        slot = jnp.where(holder == column, 0, 1)
        key = (holder * 2 + (name & 1)) * 2 + slot
        weight = combine_ref[:, k : k + 1]
        named = (lane == name) | (lane == name + experts)
        side = side + jnp.where(named, weight, 0.0)
        side = side + jnp.where(lane == key + 2 * experts, 1.0, 0.0)
    left, right = normed[:, :half], normed[:, half:]
    mine = jnp.where(c == 0, left, right)
    swap_out[:, :half] = jnp.where(c == 0, right, left)
    swap_out[:, half:] = side

    pl.semaphore_wait(barrier, len(partners))
    send(swap_out, swap_in, pair_send.at[0], pair_recv.at[0], sibling)
    send(
        down_hbm.at[0, :, pl.ds(pl.multiple_of((1 - c) * half, half), half)],
        down_v.at[c], pair_send.at[1], pair_recv.at[1], sibling,
    )
    arrived(swap_in, pair_send.at[0], pair_recv.at[0])
    other = swap_in[:, :half]
    rows = jnp.concatenate(
        [jnp.where(c == 0, mine, other), jnp.where(c == 0, other, mine)], axis=0
    ).astype(BF16)
    other_side = swap_in[:, half:]
    side = jnp.concatenate(
        [jnp.where(c == 0, side, other_side), jnp.where(c == 0, other_side, side)], axis=0
    )
    lanes = lax.broadcasted_iota(jnp.int32, side.shape, 1)
    low = (lanes >= experts) & (lanes < 2 * experts)
    side = jnp.where(low, side - side.astype(BF16).astype(F32), side).astype(BF16)
    g0[c, here, z, :, :quarter] = rows[:, :quarter]
    g0[c, here, z, :, quarter:] = side
    g1[c, here, z] = rows[:, quarter:]

    def block(q, place, step):
        return grow[q].at[c, place, lax.rem(z - step + depth, depth)]

    def to_sibling(q, kind, step):
        ref = block(q, cat[kind], step)
        send(ref, ref, sib_send.at[q, kind, step], sib_recv.at[q, kind, step], sibling)

    def spread(step):
        for q in range(2):
            ref = block(q, here, step)
            send(ref, ref, a1_send.at[q, step], a1_recv.at[q, step], near[q])
        for q in range(2):
            ref = block(q, here, step)
            send(ref, ref, a2_send.at[q, 0, step], a2_recv.at[q, 0, step], near[1 - q])
            to_sibling(q, 0, step)

    def forward(step):
        for q in range(2):
            ref = block(q, cat[1 + q], step)
            arrived(ref, a1_send.at[q, step], a1_recv.at[q, step])
            send(ref, ref, a2_send.at[q, 1, step], a2_recv.at[q, 1, step], near[1 - q])
            to_sibling(q, 1 + q, step)

    for step in range(1, depth):
        for q in range(2):
            ref = block(q, here, 0)
            send(ref, ref, z_send.at[q, step], z_recv.at[q, step], z_at(step))
    spread(0)
    for step in range(1, depth):
        for q in range(2):
            arrived(block(q, here, step), z_send.at[q, step], z_recv.at[q, step])
        spread(step)
        forward(step - 1)
    forward(depth - 1)
    for step in range(depth):
        for q in range(2):
            for j in range(2):
                kind = 3 if j == 1 else 2 - q
                arrived(block(q, cat[kind], step), a2_send.at[q, j, step], a2_recv.at[q, j, step])
                to_sibling(q, kind, step)

    all_rows = 4 * depth * 2 * tok_rows
    for copy in loads_in:
        copy.wait()

    def project(h, first):
        for q in range(2):
            block_rows = grow[q][h, :, :, :, :quarter].reshape(all_rows, quarter)
            at = pl.ds(pl.multiple_of(h * half + q * quarter, quarter), quarter)
            gate = jnp.dot(block_rows, gate_v[at, :], preferred_element_type=F32)
            up = jnp.dot(block_rows, up_v[at, :], preferred_element_type=F32)
            if first and q == 0:
                gate_acc[...] = gate
                up_acc[...] = up
            else:
                gate_acc[...] += gate
                up_acc[...] += up

    project(c, True)
    for step in range(depth):
        for q in range(2):
            for kind in range(4):
                ref = grow[q].at[1 - c, cat[kind], lax.rem(z - step + depth, depth)]
                arrived(ref, sib_send.at[q, kind, step], sib_recv.at[q, kind, step])
    project(1 - c, False)
    gate = gate_acc[...]
    hidden = gate * (1.0 / (1.0 + jnp.exp(-gate))) * up_acc[...]
    hidden_v[c] = hidden.astype(BF16)
    send(hidden_v.at[c], hidden_v.at[c], pair_send.at[2], pair_recv.at[2], sibling)

    meta = g0[c, :, :, :, quarter:].reshape(all_rows, LANES).astype(F32)
    meta_lane = lax.broadcasted_iota(jnp.int32, meta.shape, 1)
    ours = (meta_lane == chip) | (meta_lane == chip + experts)
    weights = jnp.sum(jnp.where(ours, meta, 0.0), axis=1, keepdims=True)
    gate_acc[:, :LANES] = jnp.broadcast_to(weights, (all_rows, LANES))
    totals = jnp.sum(meta, axis=0, keepdims=True)
    total_lane = lax.broadcasted_iota(jnp.int32, totals.shape, 1)
    base = 2 * experts + 2 * chip
    home_count = jnp.sum(jnp.where(total_lane == base, totals, 0.0), axis=1, keepdims=True)
    copy_count = jnp.sum(jnp.where(total_lane == base + 1, totals, 0.0), axis=1, keepdims=True)
    two = lax.broadcasted_iota(jnp.int32, (1, 2), 1)
    loads_ref[...] = jnp.where(two == 0, home_count, copy_count) / tok_rows

    arrived(down_v.at[1 - c], pair_send.at[1], pair_recv.at[1])
    arrived(hidden_v.at[1 - c], pair_send.at[2], pair_recv.at[2])
    line = depth * 2 * tok_rows

    def line_rows(ref, place):
        return ref[pl.ds(pl.multiple_of(place * line, line), line), :]

    def outputs(q, places):
        total = None
        for p in range(2):
            part = jnp.concatenate([line_rows(hidden_v.at[p], place) for place in places], axis=0)
            at = slice(q * quarter, (q + 1) * quarter)
            term = jnp.dot(part, down_v[p, :, at], preferred_element_type=F32)
            total = term if total is None else total + term
        factor = jnp.concatenate(
            [line_rows(gate_acc, place)[:, :1] for place in places], axis=0
        )
        return (total * factor).reshape(2, depth, 2 * tok_rows, quarter)

    back = (y_next, x_next)
    def first_hop(q, j, step):
        to = lax.rem(z + step, depth)
        send(
            s1.at[q, j, to], r1.at[q, j, to],
            c1_send.at[q, j, step], c1_recv.at[q, j, step], back[q],
        )

    order = list(range(1, depth)) + [0]
    for q in range(2):
        far = (cat[3], cat[2 - q])
        s1[q] = outputs(q, far).astype(BF16)
        for step in order:
            first_hop(q, 0, step)
    for q in range(2):
        own[q] = outputs(q, (cat[1 + q], here))
    for step in order:
        for q in range(2):
            to = lax.rem(z + step, depth)
            arrived(r1.at[q, 0, to], c1_send.at[q, 0, step], c1_recv.at[q, 0, step])
            s2[q, to] = (own[q, 0, to] + r1[q, 0, to].astype(F32)).astype(BF16)
            send(
                s2.at[q, to], r2.at[q, to],
                c2_send.at[q, step], c2_recv.at[q, step], back[1 - q],
            )
        for q in range(2):
            first_hop(q, 1, step)
    for step in order:
        for q in range(2):
            to = lax.rem(z + step, depth)
            arrived(r1.at[q, 1, to], c1_send.at[q, 1, step], c1_recv.at[q, 1, step])
            arrived(r2.at[q, to], c2_send.at[q, step], c2_recv.at[q, step])
            value = own[q, 1, to] + r1[q, 1, to].astype(F32) + r2[q, to].astype(F32)
            if step == 0:
                own[q, 1, to] = value
            else:
                s3[q, step] = value.astype(BF16)
                send(
                    s3.at[q, step], r3.at[q, step],
                    c3_send.at[q, step], c3_recv.at[q, step], z_at(step),
                )
    kept = []
    for q in range(2):
        value = own[q, 1, z]
        for step in range(1, depth):
            arrived(r3.at[q, step], c3_send.at[q, step], c3_recv.at[q, step])
            value = value + r3[q, step].astype(F32)
        top, bottom = value[:tok_rows], value[tok_rows:]
        f_out[q] = jnp.where(c == 0, bottom, top)
        kept.append(jnp.where(c == 0, top, bottom))
    send(f_out, f_in, pair_send.at[3], pair_recv.at[3], sibling)
    arrived(f_in, pair_send.at[3], pair_recv.at[3])
    for q in range(2):
        there = f_in[q]
        for h in range(2):
            mixed_ref[:, h * half + q * quarter : h * half + (q + 1) * quarter] = jnp.where(
                c == h, kept[q], there
            ).astype(BF16)
    for copy in sends:
        copy.wait_send()


def hand_out(mixed_in, loads_in, mixed_ref, loads_ref):
    mixed_ref[...] = mixed_in[...]
    loads_ref[...] = loads_in[...]


def fused(tokens, norm_gain, gate, up, down, chosen, choice, cols, combine):
    tok_rows, width = tokens.shape
    ff = gate.shape[2]
    depth = lax.axis_size("expert") // 2
    half, quarter, pair_rows = width // 2, width // 4, 2 * tok_rows
    rows = 4 * depth * pair_rows
    vmem = pl.BlockSpec(memory_space=pltpu.VMEM)
    smem = pl.BlockSpec(memory_space=pltpu.SMEM)
    anywhere = pl.BlockSpec(memory_space=pl.ANY)
    dma = pltpu.SemaphoreType.DMA
    mixed, loads = pl.pallas_call(
        functools.partial(fused_kernel, depth, cols.shape[1]),
        out_shape=(
            jax.ShapeDtypeStruct((tok_rows, width), BF16),
            jax.ShapeDtypeStruct((1, 2), F32),
        ),
        in_specs=[vmem, vmem, vmem, vmem, smem, vmem, anywhere, anywhere, anywhere],
        out_specs=(vmem, vmem),
        scratch_shapes=[
            pltpu.VMEM((width, ff), BF16),
            pltpu.VMEM((width, ff), BF16),
            pltpu.VMEM((2, ff, half), BF16),
            pltpu.VMEM((tok_rows, half + LANES), F32),
            pltpu.VMEM((tok_rows, half + LANES), F32),
            pltpu.VMEM((2, 4, depth, pair_rows, quarter + LANES), BF16),
            pltpu.VMEM((2, 4, depth, pair_rows, quarter), BF16),
            pltpu.VMEM((rows, ff), F32),
            pltpu.VMEM((rows, ff), F32),
            pltpu.VMEM((2, rows, ff), BF16),
            pltpu.VMEM((2, 2, depth, pair_rows, quarter), BF16),
            pltpu.VMEM((2, 2, depth, pair_rows, quarter), BF16),
            pltpu.VMEM((2, 2, depth, pair_rows, quarter), F32),
            pltpu.VMEM((2, depth, pair_rows, quarter), BF16),
            pltpu.VMEM((2, depth, pair_rows, quarter), BF16),
            pltpu.VMEM((2, depth, pair_rows, quarter), BF16),
            pltpu.VMEM((2, depth, pair_rows, quarter), BF16),
            pltpu.VMEM((2, tok_rows, quarter), F32),
            pltpu.VMEM((2, tok_rows, quarter), F32),
            dma((3,)), dma((4,)), dma((4,)),
            dma((2, depth)), dma((2, depth)), dma((2, depth)), dma((2, depth)),
            dma((2, 2, depth)), dma((2, 2, depth)), dma((2, 4, depth)), dma((2, 4, depth)),
            dma((2, 2, depth)), dma((2, 2, depth)), dma((2, depth)), dma((2, depth)),
            dma((2, depth)), dma((2, depth)),
        ],
        compiler_params=pltpu.CompilerParams(
            collective_id=0, has_side_effects=True, vmem_limit_bytes=56 * 1024 * 1024
        ),
    )(tokens, norm_gain.reshape(1, width), chosen, choice, cols, combine, gate, up, down)
    return pl.pallas_call(
        hand_out,
        out_shape=(
            jax.ShapeDtypeStruct((tok_rows, width), BF16),
            jax.ShapeDtypeStruct((1, 2), F32),
        ),
        in_specs=[vmem, vmem],
        out_specs=(vmem, vmem),
    )(mixed, loads)


def per_device(
    tokens,
    norm_gain,
    gate_weight,
    up_weight,
    down_weight,
    experts_chosen,
    replica_choice,
    replica_cols,
    combine_weight,
):
    expert_count = lax.axis_size("expert")
    dp_count = lax.axis_size("dp")
    axes = ("expert", "dp")
    if dp_count == 4 and expert_count % 2 == 0 and expert_count * 8 <= LANES:
        return fused(
            tokens, norm_gain, gate_weight, up_weight, down_weight,
            experts_chosen, replica_choice, replica_cols, combine_weight,
        )
    pair_cols = dp_count // 2
    pair_count = expert_count * pair_cols
    tok_rows = tokens.shape[0]
    values = tokens.astype(jnp.float32)
    scale = lax.rsqrt(jnp.mean(values * values, axis=1, keepdims=True) + 1e-06)
    normed = (values * scale * norm_gain).astype(jnp.bfloat16)
    counts, weights = plan(
        experts_chosen, replica_choice, replica_cols, combine_weight, pair_cols, pair_count
    )
    side = jnp.concatenate([weights, counts], axis=1)
    side = lax.all_gather(side, axes, axis=0, tiled=True)
    rows = lax.all_gather(normed, axes, axis=0, tiled=True)
    pair = lax.axis_index("expert") * pair_cols + lax.axis_index("dp") // 2
    weight = lax.dynamic_slice_in_dim(side, pair, 1, axis=1)
    served = jnp.sum(lax.dynamic_slice_in_dim(side, pair_count + 2 * pair, 2, axis=1), axis=0)
    loads = (served / jnp.float32(tok_rows))[None, :]
    gate_out = jnp.dot(rows, gate_weight[0], preferred_element_type=jnp.float32)
    up_out = jnp.dot(rows, up_weight[0], preferred_element_type=jnp.float32)
    hidden = (jax.nn.silu(gate_out) * up_out).astype(jnp.bfloat16)
    out = jnp.dot(hidden, down_weight[0], preferred_element_type=jnp.float32) * weight
    mixed = lax.psum_scatter(out, axes, scatter_dimension=0, tiled=True).astype(jnp.bfloat16)
    return (mixed, loads)


def solution(mesh):
    rows = P(("groups", "expert", "dp"), None)
    pieces = P(("expert", "dp"), None, None)
    return jax.shard_map(
        per_device,
        mesh=mesh,
        in_specs=(rows, P(), pieces, pieces, pieces, rows, rows, P(), rows),
        out_specs=(rows, rows),
        check_vma=False,
    )
```

```python
import functools

import jax
import jax.numpy as jnp
from jax import lax
from jax.experimental import pallas as pl
from jax.experimental.pallas import tpu as pltpu
from jax.sharding import PartitionSpec as P

MESH = pl.DeviceIdType.MESH
LANES = 128
BF16 = jnp.bfloat16
F32 = jnp.float32


def plan(experts_chosen, replica_choice, replica_cols, combine_weight, pair_cols, pair_count):
    rep_count = replica_cols.shape[1]
    column = experts_chosen // pair_cols
    within = experts_chosen % pair_cols
    rows_hot = within[..., None] == jnp.arange(pair_cols, dtype=jnp.int32)
    home_col = jnp.sum(jnp.where(rows_hot, replica_cols[:, 0], 0), axis=-1)
    flat_hot = (within * rep_count + replica_choice)[..., None] == jnp.arange(
        pair_cols * rep_count, dtype=jnp.int32
    )
    chosen_col = jnp.sum(jnp.where(flat_hot, replica_cols.reshape(-1), 0), axis=-1)
    holder_col = jnp.where(column == home_col, chosen_col, column)
    plan_slot = (holder_col != column).astype(jnp.int32)
    plan_key = (holder_col * pair_cols + within) * 2 + plan_slot
    keys = jnp.arange(pair_count * 2, dtype=jnp.int32)
    counts = jnp.sum((plan_key[..., None] == keys).astype(jnp.float32), axis=1)
    experts = jnp.arange(pair_count, dtype=jnp.int32)
    weights = jnp.sum(
        jnp.where(experts_chosen[..., None] == experts, combine_weight[..., None], 0.0), axis=1
    )
    return counts, weights


def fused_kernel(
    depth, rep_count, tokens_ref, gain_ref, chosen_ref, choice_ref, cols_ref, combine_ref,
    gate_hbm, up_hbm, down_hbm, mixed_ref, loads_ref,
    gate_v, up_v, down_v, swap_out, swap_in, g0, g1, gate_acc, up_acc, hidden_v,
    s1, r1, own, s2, r2, s3, r3,
    load_sem, pair_send, pair_recv, z_send, z_recv, a1_send, a1_recv, a2_send, a2_recv,
    sib_send, sib_recv, c1_send, c1_recv, c2_send, c2_recv, c3_send, c3_recv,
):
    grow = (g0, g1)
    tok_rows, width = tokens_ref.shape
    half, quarter = width // 2, width // 4
    ff = gate_v.shape[1]
    experts = depth * 4
    expert, dp = lax.axis_index("expert"), lax.axis_index("dp")
    z, y, x, c = expert // 2, expert % 2, dp // 2, dp % 2
    chip = expert * 2 + x
    here = y * 2 + x
    cat = (here, y * 2 + 1 - x, (1 - y) * 2 + x, (1 - y) * 2 + 1 - x)
    sibling = {"expert": expert, "dp": x * 2 + 1 - c}
    x_next = {"expert": expert, "dp": (1 - x) * 2 + c}
    y_next = {"expert": z * 2 + 1 - y, "dp": dp}
    near = (x_next, y_next)

    def z_at(step):
        return {"expert": lax.rem(z + step, depth) * 2 + y, "dp": dp}

    def core_at(step, core):
        return {"expert": lax.rem(z + step, depth) * 2 + y, "dp": x * 2 + core}

    sends = []

    def send(src, dst, send_sem, recv_sem, device):
        copy = pltpu.make_async_remote_copy(
            src_ref=src, dst_ref=dst, send_sem=send_sem, recv_sem=recv_sem,
            device_id=device, device_id_type=MESH,
        )
        copy.start()
        sends.append(copy)

    def arrived(ref, send_sem, recv_sem):
        pltpu.make_async_remote_copy(
            src_ref=ref, dst_ref=ref, send_sem=send_sem, recv_sem=recv_sem,
            device_id=sibling, device_id_type=MESH,
        ).wait_recv()

    loads_in = [
        pltpu.make_async_copy(gate_hbm.at[0], gate_v, load_sem.at[0]),
        pltpu.make_async_copy(up_hbm.at[0], up_v, load_sem.at[1]),
        pltpu.make_async_copy(
            down_hbm.at[0, :, pl.ds(pl.multiple_of(c * half, half), half)],
            down_v.at[c], load_sem.at[2],
        ),
    ]
    for copy in loads_in:
        copy.start()

    barrier = pltpu.get_barrier_semaphore()
    partners = [sibling, x_next, y_next] + [z_at(step) for step in range(1, depth)]
    partners += [core_at(step, 1 - c) for step in range(1, depth)]
    for partner in partners:
        pl.semaphore_signal(barrier, inc=1, device_id=partner, device_id_type=MESH)

    values = tokens_ref[...].astype(F32)
    scale = lax.rsqrt(jnp.mean(values * values, axis=1, keepdims=True) + 1e-06)
    normed = (values * scale * gain_ref[...]).astype(BF16).astype(F32)
    lane = lax.broadcasted_iota(jnp.int32, (tok_rows, LANES), 1)
    side = jnp.zeros((tok_rows, LANES), F32)
    for k in range(chosen_ref.shape[1]):
        name = chosen_ref[:, k : k + 1]
        pick = choice_ref[:, k : k + 1]
        odd = (name & 1) == 1
        home = jnp.where(odd, cols_ref[1, 0], cols_ref[0, 0])
        holder = jnp.zeros_like(name)
        for r in range(rep_count):
            holder = jnp.where(pick == r, jnp.where(odd, cols_ref[1, r], cols_ref[0, r]), holder)
        column = name >> 1
        holder = jnp.where(column == home, holder, column)
        slot = jnp.where(holder == column, 0, 1)
        key = (holder * 2 + (name & 1)) * 2 + slot
        weight = combine_ref[:, k : k + 1]
        named = (lane == name) | (lane == name + experts)
        side = side + jnp.where(named, weight, 0.0)
        side = side + jnp.where(lane == key + 2 * experts, 1.0, 0.0)
    left, right = normed[:, :half], normed[:, half:]
    mine = jnp.where(c == 0, left, right)
    swap_out[:, :half] = jnp.where(c == 0, right, left)
    swap_out[:, half:] = side

    pl.semaphore_wait(barrier, len(partners))
    send(swap_out, swap_in, pair_send.at[0], pair_recv.at[0], sibling)
    send(
        down_hbm.at[0, :, pl.ds(pl.multiple_of((1 - c) * half, half), half)],
        down_v.at[c], pair_send.at[1], pair_recv.at[1], sibling,
    )
    arrived(swap_in, pair_send.at[0], pair_recv.at[0])
    other = swap_in[:, :half]
    rows = jnp.concatenate(
        [jnp.where(c == 0, mine, other), jnp.where(c == 0, other, mine)], axis=0
    ).astype(BF16)
    other_side = swap_in[:, half:]
    side = jnp.concatenate(
        [jnp.where(c == 0, side, other_side), jnp.where(c == 0, other_side, side)], axis=0
    )
    lanes = lax.broadcasted_iota(jnp.int32, side.shape, 1)
    low = (lanes >= experts) & (lanes < 2 * experts)
    side = jnp.where(low, side - side.astype(BF16).astype(F32), side).astype(BF16)
    g0[c, here, z, :, :quarter] = rows[:, :quarter]
    g0[c, here, z, :, quarter:] = side
    g1[c, here, z] = rows[:, quarter:]

    def block(q, place, step):
        return grow[q].at[c, place, lax.rem(z - step + depth, depth)]

    def to_sibling(q, kind, step):
        ref = block(q, cat[kind], step)
        send(ref, ref, sib_send.at[q, kind, step], sib_recv.at[q, kind, step], sibling)

    def spread(step):
        for q in range(2):
            ref = block(q, here, step)
            send(ref, ref, a1_send.at[q, step], a1_recv.at[q, step], near[q])
        for q in range(2):
            ref = block(q, here, step)
            send(ref, ref, a2_send.at[q, 0, step], a2_recv.at[q, 0, step], near[1 - q])
            to_sibling(q, 0, step)

    def forward(step):
        for q in range(2):
            ref = block(q, cat[1 + q], step)
            arrived(ref, a1_send.at[q, step], a1_recv.at[q, step])
            send(ref, ref, a2_send.at[q, 1, step], a2_recv.at[q, 1, step], near[1 - q])
            to_sibling(q, 1 + q, step)

    for step in range(1, depth):
        for q in range(2):
            ref = block(q, here, 0)
            send(ref, ref, z_send.at[q, step], z_recv.at[q, step], z_at(step))
    spread(0)
    for step in range(1, depth):
        for q in range(2):
            arrived(block(q, here, step), z_send.at[q, step], z_recv.at[q, step])
        spread(step)
        forward(step - 1)
    forward(depth - 1)
    for step in range(depth):
        for q in range(2):
            for j in range(2):
                kind = 3 if j == 1 else 2 - q
                arrived(block(q, cat[kind], step), a2_send.at[q, j, step], a2_recv.at[q, j, step])
                to_sibling(q, kind, step)

    all_rows = 4 * depth * 2 * tok_rows
    for copy in loads_in:
        copy.wait()

    def project(h, first):
        for q in range(2):
            block_rows = grow[q][h, :, :, :, :quarter].reshape(all_rows, quarter)
            at = pl.ds(pl.multiple_of(h * half + q * quarter, quarter), quarter)
            gate = jnp.dot(block_rows, gate_v[at, :], preferred_element_type=F32)
            up = jnp.dot(block_rows, up_v[at, :], preferred_element_type=F32)
            if first and q == 0:
                gate_acc[...] = gate
                up_acc[...] = up
            else:
                gate_acc[...] += gate
                up_acc[...] += up

    project(c, True)
    for step in range(depth):
        for q in range(2):
            for kind in range(4):
                ref = grow[q].at[1 - c, cat[kind], lax.rem(z - step + depth, depth)]
                arrived(ref, sib_send.at[q, kind, step], sib_recv.at[q, kind, step])
    project(1 - c, False)
    gate = gate_acc[...]
    hidden = gate * (1.0 / (1.0 + jnp.exp(-gate))) * up_acc[...]
    hidden_v[c] = hidden.astype(BF16)
    send(hidden_v.at[c], hidden_v.at[c], pair_send.at[2], pair_recv.at[2], sibling)

    meta = g0[c, :, :, :, quarter:].reshape(all_rows, LANES).astype(F32)
    meta_lane = lax.broadcasted_iota(jnp.int32, meta.shape, 1)
    ours = (meta_lane == chip) | (meta_lane == chip + experts)
    weights = jnp.sum(jnp.where(ours, meta, 0.0), axis=1, keepdims=True)
    gate_acc[:, :LANES] = jnp.broadcast_to(weights, (all_rows, LANES))
    totals = jnp.sum(meta, axis=0, keepdims=True)
    total_lane = lax.broadcasted_iota(jnp.int32, totals.shape, 1)
    base = 2 * experts + 2 * chip
    home_count = jnp.sum(jnp.where(total_lane == base, totals, 0.0), axis=1, keepdims=True)
    copy_count = jnp.sum(jnp.where(total_lane == base + 1, totals, 0.0), axis=1, keepdims=True)
    two = lax.broadcasted_iota(jnp.int32, (1, 2), 1)
    loads_ref[...] = jnp.where(two == 0, home_count, copy_count) / tok_rows

    arrived(down_v.at[1 - c], pair_send.at[1], pair_recv.at[1])
    arrived(hidden_v.at[1 - c], pair_send.at[2], pair_recv.at[2])
    line = depth * 2 * tok_rows

    def line_rows(ref, place):
        return ref[pl.ds(pl.multiple_of(place * line, line), line), :]

    def outputs(q, places):
        total = None
        for p in range(2):
            part = jnp.concatenate([line_rows(hidden_v.at[p], place) for place in places], axis=0)
            at = slice(q * quarter, (q + 1) * quarter)
            term = jnp.dot(part, down_v[p, :, at], preferred_element_type=F32)
            total = term if total is None else total + term
        factor = jnp.concatenate(
            [line_rows(gate_acc, place)[:, :1] for place in places], axis=0
        )
        return (total * factor).reshape(2, depth, 2 * tok_rows, quarter)

    back = (y_next, x_next)
    def first_hop(q, j, step):
        to = lax.rem(z + step, depth)
        send(
            s1.at[q, j, to], r1.at[q, j, to],
            c1_send.at[q, j, step], c1_recv.at[q, j, step], back[q],
        )

    order = list(range(1, depth)) + [0]
    for q in range(2):
        far = (cat[3], cat[2 - q])
        s1[q] = outputs(q, far).astype(BF16)
        for step in order:
            first_hop(q, 0, step)
    for q in range(2):
        own[q] = outputs(q, (cat[1 + q], here))
    for step in order:
        for q in range(2):
            to = lax.rem(z + step, depth)
            arrived(r1.at[q, 0, to], c1_send.at[q, 0, step], c1_recv.at[q, 0, step])
            s2[q, to] = (own[q, 0, to] + r1[q, 0, to].astype(F32)).astype(BF16)
            send(
                s2.at[q, to], r2.at[q, to],
                c2_send.at[q, step], c2_recv.at[q, step], back[1 - q],
            )
        for q in range(2):
            first_hop(q, 1, step)
    for step in order:
        values = []
        for q in range(2):
            to = lax.rem(z + step, depth)
            arrived(r1.at[q, 1, to], c1_send.at[q, 1, step], c1_recv.at[q, 1, step])
            arrived(r2.at[q, to], c2_send.at[q, step], c2_recv.at[q, step])
            values.append(own[q, 1, to] + r1[q, 1, to].astype(F32) + r2[q, to].astype(F32))
        for k in range(2):
            core = c if k == 0 else 1 - c
            part = jnp.concatenate(
                [jnp.where(core == 0, v[:tok_rows], v[tok_rows:]) for v in values], axis=0
            )
            if k == 0 and step == 0:
                kept = part
            else:
                s3[k, step] = part.astype(BF16)
                send(
                    s3.at[k, step], r3.at[k, step],
                    c3_send.at[k, step], c3_recv.at[k, step], core_at(step, core),
                )
    sums = [kept, jnp.zeros_like(kept)]
    for step in order:
        for k in range(2):
            if k == 1 or step != 0:
                arrived(r3.at[k, step], c3_send.at[k, step], c3_recv.at[k, step])
                sums[k] = sums[k] + r3[k, step].astype(F32)
    for q in range(2):
        same, there = [total[q * tok_rows : (q + 1) * tok_rows] for total in sums]
        for h in range(2):
            mixed_ref[:, h * half + q * quarter : h * half + (q + 1) * quarter] = jnp.where(
                c == h, same, there
            ).astype(BF16)
    for copy in sends:
        copy.wait_send()


def hand_out(mixed_in, loads_in, mixed_ref, loads_ref):
    mixed_ref[...] = mixed_in[...]
    loads_ref[...] = loads_in[...]


def fused(tokens, norm_gain, gate, up, down, chosen, choice, cols, combine):
    tok_rows, width = tokens.shape
    ff = gate.shape[2]
    depth = lax.axis_size("expert") // 2
    half, quarter, pair_rows = width // 2, width // 4, 2 * tok_rows
    rows = 4 * depth * pair_rows
    vmem = pl.BlockSpec(memory_space=pltpu.VMEM)
    smem = pl.BlockSpec(memory_space=pltpu.SMEM)
    anywhere = pl.BlockSpec(memory_space=pl.ANY)
    dma = pltpu.SemaphoreType.DMA
    mixed, loads = pl.pallas_call(
        functools.partial(fused_kernel, depth, cols.shape[1]),
        out_shape=(
            jax.ShapeDtypeStruct((tok_rows, width), BF16),
            jax.ShapeDtypeStruct((1, 2), F32),
        ),
        in_specs=[vmem, vmem, vmem, vmem, smem, vmem, anywhere, anywhere, anywhere],
        out_specs=(vmem, vmem),
        scratch_shapes=[
            pltpu.VMEM((width, ff), BF16),
            pltpu.VMEM((width, ff), BF16),
            pltpu.VMEM((2, ff, half), BF16),
            pltpu.VMEM((tok_rows, half + LANES), F32),
            pltpu.VMEM((tok_rows, half + LANES), F32),
            pltpu.VMEM((2, 4, depth, pair_rows, quarter + LANES), BF16),
            pltpu.VMEM((2, 4, depth, pair_rows, quarter), BF16),
            pltpu.VMEM((rows, ff), F32),
            pltpu.VMEM((rows, ff), F32),
            pltpu.VMEM((2, rows, ff), BF16),
            pltpu.VMEM((2, 2, depth, pair_rows, quarter), BF16),
            pltpu.VMEM((2, 2, depth, pair_rows, quarter), BF16),
            pltpu.VMEM((2, 2, depth, pair_rows, quarter), F32),
            pltpu.VMEM((2, depth, pair_rows, quarter), BF16),
            pltpu.VMEM((2, depth, pair_rows, quarter), BF16),
            pltpu.VMEM((2, depth, pair_rows, quarter), BF16),
            pltpu.VMEM((2, depth, pair_rows, quarter), BF16),
            dma((3,)), dma((3,)), dma((3,)),
            dma((2, depth)), dma((2, depth)), dma((2, depth)), dma((2, depth)),
            dma((2, 2, depth)), dma((2, 2, depth)), dma((2, 4, depth)), dma((2, 4, depth)),
            dma((2, 2, depth)), dma((2, 2, depth)), dma((2, depth)), dma((2, depth)),
            dma((2, depth)), dma((2, depth)),
        ],
        compiler_params=pltpu.CompilerParams(
            collective_id=0, has_side_effects=True, vmem_limit_bytes=56 * 1024 * 1024
        ),
    )(tokens, norm_gain.reshape(1, width), chosen, choice, cols, combine, gate, up, down)
    return pl.pallas_call(
        hand_out,
        out_shape=(
            jax.ShapeDtypeStruct((tok_rows, width), BF16),
            jax.ShapeDtypeStruct((1, 2), F32),
        ),
        in_specs=[vmem, vmem],
        out_specs=(vmem, vmem),
    )(mixed, loads)


def per_device(
    tokens,
    norm_gain,
    gate_weight,
    up_weight,
    down_weight,
    experts_chosen,
    replica_choice,
    replica_cols,
    combine_weight,
):
    expert_count = lax.axis_size("expert")
    dp_count = lax.axis_size("dp")
    axes = ("expert", "dp")
    if dp_count == 4 and expert_count % 2 == 0 and expert_count * 8 <= LANES:
        return fused(
            tokens, norm_gain, gate_weight, up_weight, down_weight,
            experts_chosen, replica_choice, replica_cols, combine_weight,
        )
    pair_cols = dp_count // 2
    pair_count = expert_count * pair_cols
    tok_rows = tokens.shape[0]
    values = tokens.astype(jnp.float32)
    scale = lax.rsqrt(jnp.mean(values * values, axis=1, keepdims=True) + 1e-06)
    normed = (values * scale * norm_gain).astype(jnp.bfloat16)
    counts, weights = plan(
        experts_chosen, replica_choice, replica_cols, combine_weight, pair_cols, pair_count
    )
    side = jnp.concatenate([weights, counts], axis=1)
    side = lax.all_gather(side, axes, axis=0, tiled=True)
    rows = lax.all_gather(normed, axes, axis=0, tiled=True)
    pair = lax.axis_index("expert") * pair_cols + lax.axis_index("dp") // 2
    weight = lax.dynamic_slice_in_dim(side, pair, 1, axis=1)
    served = jnp.sum(lax.dynamic_slice_in_dim(side, pair_count + 2 * pair, 2, axis=1), axis=0)
    loads = (served / jnp.float32(tok_rows))[None, :]
    gate_out = jnp.dot(rows, gate_weight[0], preferred_element_type=jnp.float32)
    up_out = jnp.dot(rows, up_weight[0], preferred_element_type=jnp.float32)
    hidden = (jax.nn.silu(gate_out) * up_out).astype(jnp.bfloat16)
    out = jnp.dot(hidden, down_weight[0], preferred_element_type=jnp.float32) * weight
    mixed = lax.psum_scatter(out, axes, scatter_dimension=0, tiled=True).astype(jnp.bfloat16)
    return (mixed, loads)


def solution(mesh):
    rows = P(("groups", "expert", "dp"), None)
    pieces = P(("expert", "dp"), None, None)
    return jax.shard_map(
        per_device,
        mesh=mesh,
        in_specs=(rows, P(), pieces, pieces, pieces, rows, rows, P(), rows),
        out_specs=(rows, rows),
        check_vma=False,
    )
```
